32 devices in a mesh: section: 4 (over y, x), dp: 8 (over z, core).
Axes of the slice: x: 2, y: 2, z: 4, core: 2. Of those that a mesh axis runs over, the one named last changes fastest.
Arguments:
- tokens: bfloat16 [1024, 8192], P('dp'), may hold values from -6 to 6
- cotangent: bfloat16 [1024, 8192], P('dp'), may hold values from -6 to 6
- gains: float32 [4, 8192], P('section'), may hold values from 0.5 to 1.5
- value_projection_weight: bfloat16 [4, 8192, 1024], P('section', 'dp'), may hold values from -0.0625 to 0.0625
- output_projection_weight: bfloat16 [4, 8192, 1024], P('section', 'dp'), may hold values from -0.1875 to 0.1875
- block_adapter_ids: int32 [8], replicated, may hold values from 0 to 63
- job_adapter: int32 [8, 64], replicated, may hold values from -1 to 63, as said below
- job_slab: int32 [8, 64], replicated, may hold values from -1 to 3, as said below
- token_counts: int32 [64], replicated, may hold values from 128 to 1023
- slot_adapter_params: bfloat16 [4, 512, 36864], P('section', 'dp'), may hold values from -0.29882812 to 0.29882812
- first_moment: float32 [4, 512, 36864], P('section', 'dp'), may hold values from -6 to 6
- second_moment: float32 [4, 512, 36864], P('section', 'dp'), may hold values from 0.1 to 10
Outputs:
- new_params: bfloat16 [4, 512, 36864], P('section', 'dp')
- new_first: float32 [4, 512, 36864], P('section', 'dp')
- new_second: float32 [4, 512, 36864], P('section', 'dp')
- user_panels: bfloat16 [4, 8, 147456], P('section', 'dp')
The draws below stay inside these ranges and needn't reach their ends.
Inputs may be any that keep to these rules, and one draw needn't show every extreme that they name: `job_adapter`: row o lists the adapters of which owner o holds a slab, each once, followed by -1; the 4 slabs of every adapter are held by 4 different owners, and every slab of every adapter is held exactly once. `job_slab`: the slab held in the same entry of job_adapter; -1 exactly where job_adapter is -1.
All inputs are finite; a program needn't handle non-finite values.
Results may differ from the reference program's by a relative error of at most 0.001.
Values may be sent and summed in bfloat16 or wider, within the bound.
A program may use at most 128 MiB of HBM per device.

```python
import math
import jax
import jax.numpy as jnp
import numpy as np
from jax import lax

D = 8192
KVW = 1024
ADAPTER_RANK = 16
ADAPTERS = 64
BLOCK = 128
SECTIONS = 4
OWNERS = 8
NSLAB = 4
TOKENS = 1024
BLOCKS = 8
PARAMS = 147456
PANEL = 36864


def owner_plan(key):
    base_key = jax.random.fold_in(key, 11)
    key_center, key_offset = jax.random.split(base_key)
    center = jax.random.randint(key_center, (), 0, OWNERS)
    offsets = jax.random.randint(key_offset, (ADAPTERS,), 0, NSLAB)
    offsets = offsets.at[0].set(NSLAB - 1)
    starts = (center - offsets) % OWNERS
    owners = jnp.arange(OWNERS, dtype=jnp.int32)[:, None]
    slab_index = (owners - starts[None, :]) % OWNERS
    covered = slab_index < NSLAB
    list_rank = jnp.cumsum(covered.astype(jnp.int32), axis=1) - 1
    column = jnp.where(covered, list_rank, ADAPTERS)
    rows_grid = jnp.broadcast_to(owners, (OWNERS, ADAPTERS))
    adapter_grid = jnp.broadcast_to(jnp.arange(ADAPTERS, dtype=jnp.int32)[None, :], (OWNERS, ADAPTERS))
    empty_table = jnp.full((OWNERS, ADAPTERS), -1, jnp.int32)
    job_first = empty_table.at[rows_grid, column].set(adapter_grid, mode='drop')
    job_second = empty_table.at[rows_grid, column].set(slab_index.astype(jnp.int32), mode='drop')
    return (job_first, job_second)


def draw_job_adapter(key, part):
    return owner_plan(key)[0]


def draw_job_slab(key, part):
    return owner_plan(key)[1]


def plant(array, key, low, largest):
    spot = [jax.random.randint(jax.random.fold_in(key, axis), (), 0, length) for axis, length in enumerate(array.shape)]
    main_axis = array.shape.index(max(array.shape))
    beside = spot[:main_axis] + [(spot[main_axis] + 1) % array.shape[main_axis]] + spot[main_axis + 1:]
    return array.at[tuple(spot)].set(low).at[tuple(beside)].set(largest)


def block_levels(own_key, extent, cuts, low, largest):
    level = 1.0
    for axis_at, blocks in cuts:
        heights = jax.random.uniform(jax.random.fold_in(jax.random.fold_in(own_key, 6), axis_at), (blocks,), jnp.float32, low / len(cuts), largest / len(cuts))
        level = level * jnp.repeat(jnp.exp(heights), extent[axis_at] // blocks).reshape((-1,) + (1,) * (len(extent) - 1 - axis_at))
    return level


def rank_table(amount, lean):
    loads = [(1 << 20) // math.isqrt(rank ** lean) + 1 for rank in range(1, amount + 1)]
    scale = 1 + sum(loads) // (1 << 30)
    return np.cumsum(np.array([max(1, weight // scale) for weight in loads]))


def ranked(key, dims, amount, skew):
    grid = rank_table(amount, skew)
    lot = jax.random.randint(jax.random.fold_in(key, 1), dims, 0, int(grid[amount - 1]))
    rank = jnp.searchsorted(jnp.asarray(grid, jnp.int32), lot, side="right")
    return jax.random.permutation(jax.random.fold_in(key, 2), amount)[rank].astype(jnp.int32)


def scatter_about(own_key, extent, width, most, shards=(), kind=jnp.bfloat16):
    entries = jax.random.normal(own_key, extent, jnp.float32) * width
    if len(shards) > 0:
        entries = block_levels(own_key, extent, shards, -0.22, 0.18) * entries
    return jnp.clip(entries, min=-most, max=most).astype(kind)


def setup_inputs(seed: int = 0) -> dict:
    streams_of = jax.random.split(jax.random.key(seed), 13)
    tokens = scatter_about(streams_of[0], (TOKENS, D), 1.0, 6.0, ((0, 8),))
    cotangent = scatter_about(streams_of[1], (TOKENS, D), 1.0, 6.0, ((0, 8),))
    gains = jnp.clip(1.0 + 0.1 * jax.random.normal(streams_of[2], (SECTIONS, D), jnp.float32), 0.5, 1.5)
    value_projection_weight = scatter_about(streams_of[3], (SECTIONS, D, KVW), D ** -0.5, 0.0625, ((0, 4), (1, 8)))
    output_projection_weight = scatter_about(streams_of[4], (SECTIONS, D, KVW), KVW ** -0.5, 0.1875, ((0, 4), (1, 8)))
    block_adapter_ids = plant(ranked(streams_of[5], (BLOCKS,), ADAPTERS, 2), jax.random.fold_in(streams_of[5], 3), 0, ADAPTERS - 1).astype(jnp.int32)
    job_adapter = draw_job_adapter(jax.random.fold_in(streams_of[12], 71), 0)
    job_slab = draw_job_slab(jax.random.fold_in(streams_of[12], 71), 0)
    token_counts = plant(jax.random.randint(streams_of[8], (ADAPTERS,), BLOCK, 8 * BLOCK), jax.random.fold_in(streams_of[8], 1), BLOCK, (8 * BLOCK) - 1).astype(jnp.int32)
    slot_adapter_params = scatter_about(streams_of[9], (SECTIONS, OWNERS * ADAPTERS, PANEL), 0.05, 0.29882812, ((0, 4), (1, 8)))
    first_moment = scatter_about(streams_of[10], (SECTIONS, OWNERS * ADAPTERS, PANEL), 1.0, 6.0, ((0, 4), (1, 8)), jnp.float32)
    second_moment = jnp.clip(jnp.exp(math.log(10.0) - 4.6051702 * jax.random.uniform(streams_of[11], (SECTIONS, OWNERS * ADAPTERS, PANEL), jnp.float32) ** block_levels(streams_of[11], (SECTIONS, OWNERS * ADAPTERS, PANEL), ((0, 4), (1, 8)), -0.2, 0.2)), 0.1, 10.0)
    return {"tokens": tokens, "cotangent": cotangent, "gains": gains, "value_projection_weight": value_projection_weight, "output_projection_weight": output_projection_weight, "block_adapter_ids": block_adapter_ids, "job_adapter": job_adapter, "job_slab": job_slab, "token_counts": token_counts, "slot_adapter_params": slot_adapter_params, "first_moment": first_moment, "second_moment": second_moment}


ADAPTER_SCALE = 2.0
LEARN_RATE = 0.001
BETA_FIRST = 0.9
BETA_SECOND = 0.999
ADAM_EPS = 1e-08
FIRST_FIX = 1.0 - 0.9 ** 50 * 0.9 ** 50
SECOND_FIX = 1.0 - 0.999 ** 50 * 0.999 ** 50
NORM_EPS = 1e-05

def contract_trailing(left, right):
    return lax.dot_general(left, right, (((1,), (1,)), ((), ())), preferred_element_type=jnp.float32)

def contract_leading(left, right):
    return lax.dot_general(left, right, (((0,), (0,)), ((), ())), preferred_element_type=jnp.float32)

def norm_rows(hidden_state, gain_vector_row):
    hidden_wide = hidden_state.astype(jnp.float32)
    mean_square = lax.optimization_barrier(jnp.mean(hidden_wide * hidden_wide, axis=-1, keepdims=True))
    norm_gain_scale = lax.rsqrt(mean_square + NORM_EPS)
    normalized_rows = (hidden_wide * norm_gain_scale * gain_vector_row).astype(jnp.bfloat16)
    return (hidden_wide, norm_gain_scale, normalized_rows)

def layer_ahead_pass(hidden_state, gain_vector_row, value_complete, output_complete, adapter_down, adapter_up):
    hidden_wide, norm_gain_scale, normalized_rows = norm_rows(hidden_state, gain_vector_row)
    rank_projected = jnp.dot(normalized_rows, adapter_down, preferred_element_type=jnp.float32).astype(jnp.bfloat16)
    value_block_rows = (jnp.dot(normalized_rows, value_complete, preferred_element_type=jnp.float32) + ADAPTER_SCALE * jnp.dot(rank_projected, adapter_up, preferred_element_type=jnp.float32)).astype(jnp.bfloat16)
    output_block_rows = (hidden_wide + contract_trailing(value_block_rows, output_complete)).astype(jnp.bfloat16)
    return (output_block_rows, norm_gain_scale, normalized_rows, rank_projected)

def layer_reverse_pass(output_gradient, hidden_state, norm_gain_scale, normalized_rows, rank_projected, gain_vector_row, value_complete, output_complete, adapter_down, adapter_up):
    value_gradient = jnp.dot(output_gradient, output_complete, preferred_element_type=jnp.float32).astype(jnp.bfloat16)
    low_rank_gradient = (ADAPTER_SCALE * contract_trailing(value_gradient, adapter_up)).astype(jnp.bfloat16)
    down_gradient = contract_leading(normalized_rows, low_rank_gradient)
    up_gradient = ADAPTER_SCALE * contract_leading(rank_projected, value_gradient)
    normed_gradient = (contract_trailing(value_gradient, value_complete) + contract_trailing(low_rank_gradient, adapter_down)) * gain_vector_row
    hidden_wide = hidden_state.astype(jnp.float32)
    centred = lax.optimization_barrier(jnp.mean(hidden_wide * normed_gradient, axis=-1, keepdims=True))
    grad_in = output_gradient.astype(jnp.float32) + norm_gain_scale * normed_gradient - hidden_wide * norm_gain_scale ** 3 * centred
    return (grad_in.astype(jnp.bfloat16), down_gradient, up_gradient)

def adam_update(params_old, first_old, second_old, slot_grad, live):
    first_step = BETA_FIRST * first_old + (1.0 - BETA_FIRST) * slot_grad
    second_step = BETA_SECOND * second_old + (1.0 - BETA_SECOND) * slot_grad * slot_grad
    step_size = first_step / FIRST_FIX / (jnp.sqrt(second_step / SECOND_FIX) + ADAM_EPS)
    params_step = (params_old.astype(jnp.float32) - LEARN_RATE * step_size).astype(jnp.bfloat16)
    return (jnp.where(live, params_step, params_old), jnp.where(live, first_step, first_old), jnp.where(live, second_step, second_old))

def reference(tokens, cotangent, gains, value_projection_weight, output_projection_weight, block_adapter_ids, job_adapter, job_slab, token_counts, slot_adapter_params, first_moment, second_moment):
    flat_jobs = job_adapter.reshape(-1)
    flat_slabs = job_slab.reshape(-1)
    live = flat_jobs >= 0
    target = jnp.where(live, flat_jobs, ADAPTERS).astype(jnp.int32)
    slab_safe = jnp.where(live, flat_slabs, 0).astype(jnp.int32)
    divide_position = D * ADAPTER_RANK

    def build_lookup_table(owned):
        table = jnp.zeros((ADAPTERS + 1, NSLAB, PANEL), owned.dtype).at[target, slab_safe].set(owned)
        return table[:ADAPTERS].reshape(ADAPTERS, PARAMS)

    def divide_parameters(vectors):
        return (vectors[:, :divide_position].reshape(-1, D, ADAPTER_RANK), vectors[:, divide_position:].reshape(-1, ADAPTER_RANK, KVW))
    ahead_block_map = jax.vmap(layer_ahead_pass, in_axes=(0, None, None, None, 0, 0))
    reverse_block_map = jax.vmap(layer_reverse_pass, in_axes=(0, 0, 0, 0, 0, None, None, None, 0, 0))
    hidden_state = tokens.reshape(BLOCKS, BLOCK, D)
    residuals_kept = []
    for section_count_total in range(SECTIONS):
        adapter_down, adapter_up = divide_parameters(build_lookup_table(slot_adapter_params[section_count_total])[block_adapter_ids])
        output_block_rows, norm_gain_scale, normalized_rows, rank_projected = ahead_block_map(hidden_state, gains[section_count_total], value_projection_weight[section_count_total], output_projection_weight[section_count_total], adapter_down, adapter_up)
        residuals_kept.append((hidden_state, norm_gain_scale, normalized_rows, rank_projected, adapter_down, adapter_up))
        hidden_state = output_block_rows
    row_gradients = cotangent.reshape(BLOCKS, BLOCK, D)
    params_list, first_list, second_list, user_list = ([], [], [], [])
    counts_padded = jnp.concatenate([token_counts, jnp.ones((1,), jnp.int32)]).astype(jnp.float32)
    for section_count_total in reversed(range(SECTIONS)):
        hidden_input, norm_gain_scale, normalized_rows, rank_projected, adapter_down, adapter_up = residuals_kept[section_count_total]
        row_gradients, down_gradient, up_gradient = reverse_block_map(row_gradients, hidden_input, norm_gain_scale, normalized_rows, rank_projected, gains[section_count_total], value_projection_weight[section_count_total], output_projection_weight[section_count_total], adapter_down, adapter_up)
        block_grads = jnp.concatenate([down_gradient.reshape(BLOCKS, -1), up_gradient.reshape(BLOCKS, -1)], axis=1)
        adapter_grads = jax.ops.segment_sum(block_grads, block_adapter_ids, num_segments=ADAPTERS)
        adapter_grads = jnp.concatenate([adapter_grads.reshape(ADAPTERS, NSLAB, PANEL), jnp.zeros((1, NSLAB, PANEL), jnp.float32)], axis=0)
        slot_grad = adapter_grads[target, slab_safe] / counts_padded[target][:, None]
        params_new, first_new, second_new = adam_update(slot_adapter_params[section_count_total], first_moment[section_count_total], second_moment[section_count_total], slot_grad, live[:, None])
        params_list.append(params_new)
        first_list.append(first_new)
        second_list.append(second_new)
        user_list.append(build_lookup_table(params_new)[block_adapter_ids])
    order = list(reversed(range(SECTIONS)))
    return (jnp.stack([params_list[i] for i in order]), jnp.stack([first_list[i] for i in order]), jnp.stack([second_list[i] for i in order]), jnp.stack([user_list[i] for i in order]))
```

```python
import functools

import jax
import jax.numpy as jnp
from jax import lax
from jax.experimental import pallas as pl
from jax.experimental.pallas import tpu as pltpu
from jax.sharding import PartitionSpec as P

ADAPTER_RANK = 16
MROWS = 16
LANES = 128


ADAPTER_SCALE = 2.0
LEARN_RATE = 0.001
BETA_FIRST = 0.9
BETA_SECOND = 0.999
ADAM_EPS = 1e-08
FIRST_FIX = 1.0 - 0.9**50 * 0.9**50
SECOND_FIX = 1.0 - 0.999**50 * 0.999**50
NORM_EPS = 1e-05
MESH = pl.DeviceIdType.MESH
BF = jnp.bfloat16
F32 = jnp.float32


def dot_nt(left, right):
    return lax.dot_general(left, right, (((1,), (1,)), ((), ())), preferred_element_type=F32)


def dot_tn(left, right):
    return lax.dot_general(left, right, (((0,), (0,)), ((), ())), preferred_element_type=F32)


def dot_nn(left, right):
    return jnp.dot(left, right, preferred_element_type=F32)


def layers_kernel(
    dims,
    tok,
    cot,
    gain,
    vw,
    ow,
    aw,
    bw,
    mask,
    fold,
    h,
    val,
    gv,
    gl,
    dh,
    snd_f,
    pr_f,
    mid_f,
    rs_f,
    snd_b,
    pr_b,
    mid_b,
    rs_b,
    h_out,
    dh_out,
    sem_f,
    sem_b,
    h_sem,
    dh_sem,
    tok_sem,
    cot_sem,
    send_sem,
):
    sections, n, micros, q, features, width = dims
    hz = n // 2
    rows = n * q
    half = rows // 2
    hidden = n * width
    s = lax.axis_index("section")
    j = lax.axis_index("dp")
    z = j // 2
    c = lax.rem(j, 2)
    peer = j + 1 - 2 * c
    last = sections - 1

    barrier = pltpu.get_barrier_semaphore()

    def greet(k, carry):
        pl.semaphore_signal(
            barrier, inc=1, device_id={"dp": lax.rem(j + k, n)}, device_id_type=MESH
        )
        return carry

    lax.fori_loop(1, n, greet, 0)

    @pl.when(s > 0)
    def _():
        pl.semaphore_signal(barrier, inc=1, device_id={"section": s - 1}, device_id_type=MESH)

    @pl.when(s < last)
    def _():
        pl.semaphore_signal(barrier, inc=1, device_id={"section": s + 1}, device_id_type=MESH)

    beside = jnp.where(s > 0, 1, 0) + jnp.where(s < last, 1, 0)
    pl.semaphore_wait(barrier, n - 1 + beside)

    def remote(source, target, send, recv, device):
        return pltpu.make_async_remote_copy(
            src_ref=source,
            dst_ref=target,
            send_sem=send,
            recv_sem=recv,
            device_id=device,
            device_id_type=MESH,
        )

    def wait_bytes(ref, sem):
        pltpu.make_async_copy(ref, ref, sem).wait()

    def spread(source, target, sem, sent, m):
        mine = pl.ds(pl.multiple_of(m * q, q), q)
        place = pl.ds(pl.multiple_of(j * q, q), q)

        def one(k, carry):
            to = lax.rem(j + k, n)
            columns = pl.ds(pl.multiple_of(to * width, width), width)
            remote(
                source.at[mine, columns], target.at[m, place], sent, sem.at[m], {"dp": to}
            ).start()
            return carry

        lax.fori_loop(1, n, one, 0)
        target[m, place, :] = source[mine, pl.ds(pl.multiple_of(j * width, width), width)]

    def spread_wait(target, sem, m):
        wait_bytes(target.at[m, pl.ds(0, (n - 1) * q)], sem.at[m])

    class Reduce:
        def __init__(self, snd, pr, mid, rs, out, sem, middle, finish):
            self.snd, self.pr, self.mid, self.rs = snd, pr, mid, rs
            self.out, self.sem, self.middle, self.finish = out, sem, middle, finish
            self.own = pl.ds(pl.multiple_of(c * half, half), half)
            self.other = pl.ds(pl.multiple_of((1 - c) * half, half), half)
            self.chunk = pl.ds(pl.multiple_of(c * half + z * q, q), q)

        def pair(self):
            return remote(
                self.snd.at[self.other], self.pr, self.sem.at[0], self.sem.at[1], {"dp": peer}
            )

        def scatter(self):
            self.pair().wait_recv()
            total = self.snd[self.own, :].astype(F32) + self.pr[...].astype(F32)
            self.mid[...] = self.middle(total)
            for k in range(1, hz):
                to = lax.rem(z + k, hz)
                remote(
                    self.mid.at[pl.ds(pl.multiple_of(to * q, q), q)],
                    self.rs.at[z],
                    self.sem.at[2],
                    self.sem.at[3],
                    {"dp": 2 * to + c},
                ).start()
            self.rs[z] = self.mid[pl.ds(pl.multiple_of(z * q, q), q), :]

        def gather(self, m):
            if hz > 1:
                wait_bytes(self.rs.at[pl.ds(0, hz - 1)], self.sem.at[3])
            total = self.rs[0].astype(F32)
            for k in range(1, hz):
                total = total + self.rs[k].astype(F32)
            self.out[m, self.chunk, :] = self.finish(total)
            for k in range(1, hz):
                to = lax.rem(z + k, hz)
                remote(
                    self.out.at[m, self.chunk],
                    self.out.at[m, self.chunk],
                    self.sem.at[4],
                    self.sem.at[5],
                    {"dp": 2 * to + c},
                ).start()

        def share(self, m):
            if hz > 1:
                wait_bytes(self.out.at[m, pl.ds(0, (hz - 1) * q)], self.sem.at[5])
            remote(
                self.out.at[m, self.own],
                self.out.at[m, self.own],
                self.sem.at[6],
                self.sem.at[7],
                {"dp": peer},
            ).start()

        def arrive(self, m):
            wait_bytes(self.out.at[m, pl.ds(0, half)], self.sem.at[7])

        def drain(self, m):
            self.pair().wait_send()
            if hz > 1:
                wait_bytes(self.mid.at[pl.ds(0, (hz - 1) * q)], self.sem.at[2])
                wait_bytes(self.out.at[m, pl.ds(0, (hz - 1) * q)], self.sem.at[4])
            wait_bytes(self.out.at[m, pl.ds(0, half)], self.sem.at[6])

    def with_stat(tail, stat):
        spot = lax.broadcasted_iota(jnp.int32, tail.shape, 1)
        high = stat.astype(BF).astype(F32)
        rest = stat - high
        return jnp.where(
            spot < ADAPTER_RANK,
            tail,
            jnp.where(
                spot == ADAPTER_RANK, high, jnp.where(spot == ADAPTER_RANK + 1, rest, 0.0)
            ),
        ).astype(BF)

    def stat_of(tail):
        spot = lax.broadcasted_iota(jnp.int32, tail.shape, 1)
        inside = (spot == ADAPTER_RANK) | (spot == ADAPTER_RANK + 1)
        return jnp.sum(jnp.where(inside, tail, 0.0), axis=1, keepdims=True)

    def middle_f(total):
        tail = total[:, features:]
        return jnp.concatenate(
            [total[:, :features].astype(BF), with_stat(tail, stat_of(tail))], axis=1
        )

    def finish_f(total):
        tail = total[:, features:]
        scale = lax.rsqrt(stat_of(tail) / hidden + NORM_EPS)
        return jnp.concatenate(
            [(total[:, :features] * scale).astype(BF), with_stat(tail * scale, scale)], axis=1
        )

    def plain(total):
        return total.astype(BF)

    ahead = Reduce(snd_f, pr_f, mid_f, rs_f, val, sem_f, middle_f, finish_f)
    back = Reduce(snd_b, pr_b, mid_b, rs_b, gv, sem_b, plain, plain)

    def wide_low(tail):
        spread_low = dot_nt(tail, fold[...])
        return jnp.where(mask[...] > 0, spread_low, 0.0).astype(BF)

    def ahead_start(m):
        @pl.when(s == 0)
        def _():
            spread_wait(h, tok_sem, m)

        @pl.when(s > 0)
        def _():
            wait_bytes(h.at[m], h_sem.at[m])

        wide = h[m].astype(F32)
        scaled = (wide * gain[...]).astype(BF)
        snd_f[:, :features] = dot_nn(scaled, vw[...]).astype(BF)
        low = jnp.where(mask[...] > 0, dot_nn(scaled, aw[...]), 0.0).astype(BF)
        squares = jnp.sum(wide * wide, axis=1, keepdims=True)
        snd_f[:, features:] = with_stat(dot_nn(low, fold[...]), squares)
        ahead.pair().start()

    def ahead_end(m):
        ahead.arrive(m)

        @pl.when(s < last)
        def _():
            low = wide_low(val[m, :, features:])
            value = (
                val[m, :, :features].astype(F32) + ADAPTER_SCALE * dot_nn(low, bw[...])
            ).astype(BF)
            result = (h[m].astype(F32) + dot_nt(value, ow[...])).astype(BF)

            @pl.when(m > 0)
            def _():
                wait_bytes(h_out, send_sem.at[0])

            h_out[...] = result
            remote(
                h_out, h.at[m], send_sem.at[0], h_sem.at[m], {"section": s + 1}
            ).start()

        ahead.drain(m)

    def back_start(m):
        @pl.when(s == last)
        def _():
            spread_wait(dh, cot_sem, m)

        @pl.when(s < last)
        def _():
            wait_bytes(dh.at[m], dh_sem.at[m])

        snd_b[...] = dot_nn(dh[m], ow[...]).astype(BF)
        back.pair().start()

    def back_end(m):
        back.arrive(m)
        grad_value = gv[m]
        grad_low = jnp.where(
            mask[...] > 0, ADAPTER_SCALE * dot_nt(grad_value, bw[...]), 0.0
        ).astype(BF)
        gl[m] = grad_low

        @pl.when(s > 0)
        def _():
            tail = val[m, :, features:]
            scale = stat_of(tail.astype(F32))
            low = wide_low(tail)
            inner = jnp.sum(
                grad_value.astype(F32) * val[m, :, :features].astype(F32), axis=1, keepdims=True
            ) + jnp.sum(grad_low.astype(F32) * low.astype(F32), axis=1, keepdims=True)
            norm_grad = (dot_nt(grad_value, vw[...]) + dot_nt(grad_low, aw[...])) * gain[...]
            result = (
                dh[m].astype(F32)
                + scale * norm_grad
                - h[m].astype(F32) * (scale * scale * inner / hidden)
            ).astype(BF)

            @pl.when(m > 0)
            def _():
                wait_bytes(dh_out, send_sem.at[1])

            dh_out[...] = result
            remote(
                dh_out, dh.at[m], send_sem.at[1], dh_sem.at[m], {"section": s - 1}
            ).start()

        back.drain(m)

    @pl.when(s == 0)
    def _():
        for m in range(min(2, micros)):
            spread(tok, h, tok_sem, send_sem.at[2], m)

    def step(t, carry):
        m_f = t - s
        m_b = t - (2 * sections - 1 - s)
        on_f = (m_f >= 0) & (m_f < micros)
        on_b = (m_b >= 0) & (m_b < micros)

        @pl.when((s == 0) & (t + 2 < micros))
        def _():
            spread(tok, h, tok_sem, send_sem.at[2], t + 2)

        @pl.when((s == last) & (t < micros))
        def _():
            spread(cot, dh, cot_sem, send_sem.at[3], t)

        pl.when(on_b)(lambda: back_start(m_b))
        pl.when(on_f)(lambda: ahead_start(m_f))
        pl.when(on_b)(lambda: back.scatter())
        pl.when(on_f)(lambda: ahead.scatter())
        pl.when(on_b)(lambda: back.gather(m_b))
        pl.when(on_f)(lambda: ahead.gather(m_f))
        pl.when(on_b)(lambda: back.share(m_b))
        pl.when(on_f)(lambda: ahead.share(m_f))
        pl.when(on_b)(lambda: back_end(m_b))
        pl.when(on_f)(lambda: ahead_end(m_f))
        return carry

    lax.fori_loop(0, micros + 2 * sections - 1, step, 0)

    @pl.when(s < last)
    def _():
        wait_bytes(h_out, send_sem.at[0])

    @pl.when(s > 0)
    def _():
        wait_bytes(dh_out, send_sem.at[1])

    @pl.when(s == 0)
    def _():
        wait_bytes(tok.at[:, pl.ds(0, (n - 1) * width)], send_sem.at[2])

    @pl.when(s == last)
    def _():
        wait_bytes(cot.at[:, pl.ds(0, (n - 1) * width)], send_sem.at[3])


def run_layers(tokens, cotangent, gain, vw, ow, aw, bw, mask, fold):
    sections, n = lax.axis_size("section"), lax.axis_size("dp")
    q = MROWS
    width, features = vw.shape
    ranks = aw.shape[1]
    micros = tokens.shape[0] // q
    rows = n * q
    wide = features + LANES
    vmem = pl.BlockSpec(memory_space=pltpu.VMEM)
    dma = pltpu.SemaphoreType.DMA
    dims = (sections, n, micros, q, features, width)
    return pl.pallas_call(
        functools.partial(layers_kernel, dims),
        out_shape=(
            jax.ShapeDtypeStruct((micros, rows, width), BF),
            jax.ShapeDtypeStruct((micros, rows, wide), BF),
            jax.ShapeDtypeStruct((micros, rows, features), BF),
            jax.ShapeDtypeStruct((micros, rows, ranks), BF),
        ),
        in_specs=[vmem] * 9,
        out_specs=(vmem,) * 4,
        scratch_shapes=[
            pltpu.VMEM((micros, rows, width), BF),
            pltpu.VMEM((rows, wide), BF),
            pltpu.VMEM((rows // 2, wide), BF),
            pltpu.VMEM((rows // 2, wide), BF),
            pltpu.VMEM((n // 2, q, wide), BF),
            pltpu.VMEM((rows, features), BF),
            pltpu.VMEM((rows // 2, features), BF),
            pltpu.VMEM((rows // 2, features), BF),
            pltpu.VMEM((n // 2, q, features), BF),
            pltpu.VMEM((rows, width), BF),
            pltpu.VMEM((rows, width), BF),
            dma((8,)),
            dma((8,)),
            dma((micros,)),
            dma((micros,)),
            dma((micros,)),
            dma((micros,)),
            dma((4,)),
        ],
        compiler_params=pltpu.CompilerParams(
            collective_id=0, has_side_effects=True, vmem_limit_bytes=58 * 1024 * 1024
        ),
    )(tokens, cotangent, gain, vw, ow, aw, bw, mask, fold)


def adam_update(params_old, first_old, second_old, slot_grad, live):
    first_step = BETA_FIRST * first_old + (1.0 - BETA_FIRST) * slot_grad
    second_step = BETA_SECOND * second_old + (1.0 - BETA_SECOND) * slot_grad * slot_grad
    step_size = first_step / FIRST_FIX / (jnp.sqrt(second_step / SECOND_FIX) + ADAM_EPS)
    params_step = (params_old.astype(jnp.float32) - LEARN_RATE * step_size).astype(jnp.bfloat16)
    return (
        jnp.where(live, params_step, params_old),
        jnp.where(live, first_step, first_old),
        jnp.where(live, second_step, second_old),
    )


def on_device(
    tokens,
    cotangent,
    gains,
    value_projection_weight,
    output_projection_weight,
    block_adapter_ids,
    job_adapter,
    job_slab,
    token_counts,
    slot_adapter_params,
    first_moment,
    second_moment,
):
    section_index = lax.axis_index("section")
    owner_index = lax.axis_index("dp")
    section_total = lax.axis_size("section")
    owner_total = lax.axis_size("dp")
    tok_dev, hidden_width = tokens.shape
    value_feature_width = value_projection_weight.shape[2]
    panel_width = slot_adapter_params.shape[2]
    slab_count = owner_total // 2
    block_total = block_adapter_ids.shape[0]
    local_blocks = block_total // owner_total
    block_rows = tok_dev // local_blocks
    adapter_total = token_counts.shape[0]
    divide_position = hidden_width * ADAPTER_RANK
    width = hidden_width // owner_total
    gain = lax.dynamic_slice_in_dim(gains, owner_index * width, width, axis=1)
    my_jobs = lax.dynamic_index_in_dim(job_adapter, owner_index, 0, keepdims=False)
    my_blocks = lax.dynamic_slice_in_dim(
        block_adapter_ids, owner_index * local_blocks, local_blocks
    )
    slab_ids = jnp.arange(slab_count, dtype=jnp.int32)
    matching = (job_adapter[None, None] == my_blocks[:, None, None, None]) & (
        job_slab[None, None] == slab_ids[None, :, None, None]
    )
    owner_ids = jnp.arange(owner_total, dtype=jnp.int32)
    source_owner = jnp.sum(jnp.where(matching, owner_ids[None, None, :, None], 0), axis=(2, 3))
    own_select = (block_adapter_ids[:, None] == my_jobs[None, :]) & (my_jobs[None, :] >= 0)
    slot_rows = jnp.arange(local_blocks, dtype=jnp.int32)[:, None]

    def hand_out(owned):
        picked = jnp.dot(own_select.astype(jnp.bfloat16), owned, preferred_element_type=jnp.float32)
        return picked.astype(jnp.bfloat16).reshape(owner_total, local_blocks, panel_width)

    def assemble(arrived):
        gathered_slabs = arrived[source_owner, slot_rows]
        return gathered_slabs.reshape(local_blocks, slab_count * panel_width)

    ranks = block_total * ADAPTER_RANK
    my_slabs = lax.dynamic_index_in_dim(job_slab, owner_index, 0, keepdims=False)
    held_slab = jnp.max(jnp.where(own_select, my_slabs[None, :], -1), axis=1)
    held = held_slab[:, None] == slab_ids[None, :]
    picked = hand_out(slot_adapter_params[0]).reshape(block_total, 1, panel_width)
    padded = jnp.where(held[:, :, None], picked, jnp.zeros((), BF)).reshape(
        block_total, slab_count * panel_width
    )
    down_part = jnp.transpose(
        padded[:, :divide_position].reshape(block_total, owner_total, width * ADAPTER_RANK),
        (1, 0, 2),
    )
    adapter_down = lax.psum_scatter(down_part, "dp", scatter_dimension=0, tiled=False)
    adapter_up = lax.psum(padded[:, divide_position:], "dp").reshape(ranks, value_feature_width)
    adapter_down = jnp.transpose(
        adapter_down.reshape(block_total, width, ADAPTER_RANK), (1, 0, 2)
    ).reshape(width, ranks)
    rows = owner_total * MROWS
    mask = (
        jnp.arange(rows, dtype=jnp.int32)[:, None] // MROWS
        == jnp.arange(ranks, dtype=jnp.int32)[None, :] // ADAPTER_RANK
    )
    fold = (
        jnp.arange(ranks, dtype=jnp.int32)[:, None] % ADAPTER_RANK
        == jnp.arange(LANES, dtype=jnp.int32)[None, :]
    ).astype(BF)
    hidden, val, grad_value, grad_low = run_layers(
        tokens,
        cotangent,
        gain,
        value_projection_weight[0],
        output_projection_weight[0],
        adapter_down,
        adapter_up,
        mask.astype(F32),
        fold,
    )
    total_rows = hidden.shape[0] * rows
    tail = val[:, :, value_feature_width:]
    scale = tail[:, :, ADAPTER_RANK].astype(F32) + tail[:, :, ADAPTER_RANK + 1].astype(F32)
    normed = (hidden.astype(F32) * scale[:, :, None] * gain[0]).astype(BF)
    low = jnp.where(
        mask, jnp.tile(tail[:, :, :ADAPTER_RANK], (1, 1, block_total)), jnp.zeros((), BF)
    )
    down_grads = dot_tn(
        normed.reshape(total_rows, width), grad_low.reshape(total_rows, ranks)
    ).astype(BF)
    up_grads = (
        ADAPTER_SCALE
        * dot_tn(
            low.reshape(total_rows, ranks), grad_value.reshape(total_rows, value_feature_width)
        )
    ).astype(BF)
    down_grads = jnp.transpose(
        down_grads.reshape(width, block_total, ADAPTER_RANK), (1, 0, 2)
    ).reshape(block_total, width * ADAPTER_RANK)
    down_grads = lax.all_gather(down_grads, "dp", axis=1, tiled=True)
    block_grads = jnp.concatenate(
        [down_grads, up_grads.reshape(block_total, ADAPTER_RANK * value_feature_width)], axis=1
    ).reshape(block_total, slab_count, panel_width)
    arrived = jnp.sum(
        jnp.where(held[:, :, None], block_grads.astype(F32), 0.0), axis=1
    ).astype(BF)
    summed = dot_tn(own_select.astype(BF), arrived)
    live = my_jobs >= 0
    adapter_ids = jnp.arange(adapter_total, dtype=jnp.int32)
    slot_counts = jnp.sum(
        jnp.where(adapter_ids[None, :] == my_jobs[:, None], token_counts[None, :], 0), axis=1
    )
    slot_counts = jnp.where(live, slot_counts, 1)
    slot_grad = summed / slot_counts.astype(jnp.float32)[:, None]
    params_new, first_new, second_new = adam_update(
        slot_adapter_params[0], first_moment[0], second_moment[0], slot_grad, live[:, None]
    )
    returned = assemble(
        lax.all_to_all(hand_out(params_new), "dp", split_axis=0, concat_axis=0, tiled=True)
    )
    return (params_new[None], first_new[None], second_new[None], returned[None])


def solution(mesh):
    return jax.shard_map(
        on_device,
        mesh=mesh,
        in_specs=(
            P("dp", None),
            P("dp", None),
            P("section", None),
            P("section", "dp", None),
            P("section", "dp", None),
            P(),
            P(),
            P(),
            P(),
            P("section", "dp", None),
            P("section", "dp", None),
            P("section", "dp", None),
        ),
        out_specs=(
            P("section", "dp", None),
            P("section", "dp", None),
            P("section", "dp", None),
            P("section", "dp", None),
        ),
        check_vma=False,
    )
```

```python
import functools

import jax
import jax.numpy as jnp
from jax import lax
from jax.experimental import pallas as pl
from jax.experimental.pallas import tpu as pltpu
from jax.sharding import PartitionSpec as P

ADAPTER_RANK = 16
MROWS = 16
LANES = 128


ADAPTER_SCALE = 2.0
LEARN_RATE = 0.001
BETA_FIRST = 0.9
BETA_SECOND = 0.999
ADAM_EPS = 1e-08
FIRST_FIX = 1.0 - 0.9**50 * 0.9**50
SECOND_FIX = 1.0 - 0.999**50 * 0.999**50
NORM_EPS = 1e-05
MESH = pl.DeviceIdType.MESH
BF = jnp.bfloat16
F32 = jnp.float32


def dot_nt(left, right):
    return lax.dot_general(left, right, (((1,), (1,)), ((), ())), preferred_element_type=F32)


def dot_tn(left, right):
    return lax.dot_general(left, right, (((0,), (0,)), ((), ())), preferred_element_type=F32)


def dot_nn(left, right):
    return jnp.dot(left, right, preferred_element_type=F32)


def layers_kernel(
    dims,
    tok,
    cot,
    gain,
    vw,
    ow,
    aw,
    bpart,
    mask,
    fold,
    h,
    val,
    gv,
    gl,
    dh,
    bw,
    snd_f,
    pr_f,
    mid_f,
    rs_f,
    snd_b,
    pr_b,
    mid_b,
    rs_b,
    h_out,
    dh_out,
    sem_f,
    sem_b,
    h_sem,
    dh_sem,
    tok_sem,
    cot_sem,
    up_sem,
    send_sem,
):
    sections, n, micros, q, features, width = dims
    hz = n // 2
    rows = n * q
    half = rows // 2
    hidden = n * width
    s = lax.axis_index("section")
    j = lax.axis_index("dp")
    z = j // 2
    c = lax.rem(j, 2)
    peer = j + 1 - 2 * c
    last = sections - 1

    barrier = pltpu.get_barrier_semaphore()

    def greet(k, carry):
        pl.semaphore_signal(
            barrier, inc=1, device_id={"dp": lax.rem(j + k, n)}, device_id_type=MESH
        )
        return carry

    lax.fori_loop(1, n, greet, 0)

    @pl.when(s > 0)
    def _():
        pl.semaphore_signal(barrier, inc=1, device_id={"section": s - 1}, device_id_type=MESH)

    @pl.when(s < last)
    def _():
        pl.semaphore_signal(barrier, inc=1, device_id={"section": s + 1}, device_id_type=MESH)

    beside = jnp.where(s > 0, 1, 0) + jnp.where(s < last, 1, 0)
    pl.semaphore_wait(barrier, n - 1 + beside)

    def remote(source, target, send, recv, device):
        return pltpu.make_async_remote_copy(
            src_ref=source,
            dst_ref=target,
            send_sem=send,
            recv_sem=recv,
            device_id=device,
            device_id_type=MESH,
        )

    def wait_bytes(ref, sem):
        pltpu.make_async_copy(ref, ref, sem).wait()

    def spread(source, target, sem, sent, m):
        mine = pl.ds(pl.multiple_of(m * q, q), q)
        place = pl.ds(pl.multiple_of(j * q, q), q)

        def one(k, carry):
            to = lax.rem(j + k, n)
            columns = pl.ds(pl.multiple_of(to * width, width), width)
            remote(
                source.at[mine, columns], target.at[m, place], sent, sem.at[m], {"dp": to}
            ).start()
            return carry

        lax.fori_loop(1, n, one, 0)
        target[m, place, :] = source[mine, pl.ds(pl.multiple_of(j * width, width), width)]

    def spread_wait(target, sem, m):
        wait_bytes(target.at[m, pl.ds(0, (n - 1) * q)], sem.at[m])

    class Reduce:
        def __init__(self, snd, pr, mid, rs, out, sem, middle, finish):
            self.snd, self.pr, self.mid, self.rs = snd, pr, mid, rs
            self.out, self.sem, self.middle, self.finish = out, sem, middle, finish
            self.own = pl.ds(pl.multiple_of(c * half, half), half)
            self.other = pl.ds(pl.multiple_of((1 - c) * half, half), half)
            self.chunk = pl.ds(pl.multiple_of(c * half + z * q, q), q)

        def pair(self):
            return remote(
                self.snd.at[self.other], self.pr, self.sem.at[0], self.sem.at[1], {"dp": peer}
            )

        def scatter(self):
            self.pair().wait_recv()
            total = self.snd[self.own, :].astype(F32) + self.pr[...].astype(F32)
            self.mid[...] = self.middle(total)
            for k in range(1, hz):
                to = lax.rem(z + k, hz)
                remote(
                    self.mid.at[pl.ds(pl.multiple_of(to * q, q), q)],
                    self.rs.at[z],
                    self.sem.at[2],
                    self.sem.at[3],
                    {"dp": 2 * to + c},
                ).start()
            self.rs[z] = self.mid[pl.ds(pl.multiple_of(z * q, q), q), :]

        def gather(self, m):
            if hz > 1:
                wait_bytes(self.rs.at[pl.ds(0, hz - 1)], self.sem.at[3])
            total = self.rs[0].astype(F32)
            for k in range(1, hz):
                total = total + self.rs[k].astype(F32)
            self.out[m, self.chunk, :] = self.finish(total)
            for k in range(1, hz):
                to = lax.rem(z + k, hz)
                remote(
                    self.out.at[m, self.chunk],
                    self.out.at[m, self.chunk],
                    self.sem.at[4],
                    self.sem.at[5],
                    {"dp": 2 * to + c},
                ).start()

        def share(self, m):
            if hz > 1:
                wait_bytes(self.out.at[m, pl.ds(0, (hz - 1) * q)], self.sem.at[5])
            remote(
                self.out.at[m, self.own],
                self.out.at[m, self.own],
                self.sem.at[6],
                self.sem.at[7],
                {"dp": peer},
            ).start()

        def arrive(self, m):
            wait_bytes(self.out.at[m, pl.ds(0, half)], self.sem.at[7])

        def drain(self, m):
            self.pair().wait_send()
            if hz > 1:
                wait_bytes(self.mid.at[pl.ds(0, (hz - 1) * q)], self.sem.at[2])
                wait_bytes(self.out.at[m, pl.ds(0, (hz - 1) * q)], self.sem.at[4])
            wait_bytes(self.out.at[m, pl.ds(0, half)], self.sem.at[6])

    def with_stat(tail, stat):
        spot = lax.broadcasted_iota(jnp.int32, tail.shape, 1)
        high = stat.astype(BF).astype(F32)
        rest = stat - high
        return jnp.where(
            spot < ADAPTER_RANK,
            tail,
            jnp.where(
                spot == ADAPTER_RANK, high, jnp.where(spot == ADAPTER_RANK + 1, rest, 0.0)
            ),
        ).astype(BF)

    def stat_of(tail):
        spot = lax.broadcasted_iota(jnp.int32, tail.shape, 1)
        inside = (spot == ADAPTER_RANK) | (spot == ADAPTER_RANK + 1)
        return jnp.sum(jnp.where(inside, tail, 0.0), axis=1, keepdims=True)

    def middle_f(total):
        tail = total[:, features:]
        return jnp.concatenate(
            [total[:, :features].astype(BF), with_stat(tail, stat_of(tail))], axis=1
        )

    def finish_f(total):
        tail = total[:, features:]
        scale = lax.rsqrt(stat_of(tail) / hidden + NORM_EPS)
        return jnp.concatenate(
            [(total[:, :features] * scale).astype(BF), with_stat(tail * scale, scale)], axis=1
        )

    def plain(total):
        return total.astype(BF)

    ahead = Reduce(snd_f, pr_f, mid_f, rs_f, val, sem_f, middle_f, finish_f)
    back = Reduce(snd_b, pr_b, mid_b, rs_b, gv, sem_b, plain, plain)

    def wide_low(tail):
        spread_low = dot_nt(tail, fold[...])
        return jnp.where(mask[...] > 0, spread_low, 0.0).astype(BF)

    def ahead_start(m):
        @pl.when(s == 0)
        def _():
            spread_wait(h, tok_sem, m)

        @pl.when(s > 0)
        def _():
            wait_bytes(h.at[m], h_sem.at[m])

        wide = h[m].astype(F32)
        scaled = (wide * gain[...]).astype(BF)
        snd_f[:, :features] = dot_nn(scaled, vw[...]).astype(BF)
        low = jnp.where(mask[...] > 0, dot_nn(scaled, aw[...]), 0.0).astype(BF)
        squares = jnp.sum(wide * wide, axis=1, keepdims=True)
        snd_f[:, features:] = with_stat(dot_nn(low, fold[...]), squares)
        ahead.pair().start()

    def ahead_end(m):
        ahead.arrive(m)

        @pl.when(s < last)
        def _():
            low = wide_low(val[m, :, features:])
            value = (
                val[m, :, :features].astype(F32) + ADAPTER_SCALE * dot_nn(low, bw[...])
            ).astype(BF)
            result = (h[m].astype(F32) + dot_nt(value, ow[...])).astype(BF)

            @pl.when(m > 0)
            def _():
                wait_bytes(h_out, send_sem.at[0])

            h_out[...] = result
            remote(
                h_out, h.at[m], send_sem.at[0], h_sem.at[m], {"section": s + 1}
            ).start()

        ahead.drain(m)

    def back_start(m):
        @pl.when(s == last)
        def _():
            spread_wait(dh, cot_sem, m)

        @pl.when(s < last)
        def _():
            wait_bytes(dh.at[m], dh_sem.at[m])

        snd_b[...] = dot_nn(dh[m], ow[...]).astype(BF)
        back.pair().start()

    def back_end(m):
        back.arrive(m)
        grad_value = gv[m]
        grad_low = jnp.where(
            mask[...] > 0, ADAPTER_SCALE * dot_nt(grad_value, bw[...]), 0.0
        ).astype(BF)
        gl[m] = grad_low

        @pl.when(s > 0)
        def _():
            tail = val[m, :, features:]
            scale = stat_of(tail.astype(F32))
            low = wide_low(tail)
            inner = jnp.sum(
                grad_value.astype(F32) * val[m, :, :features].astype(F32), axis=1, keepdims=True
            ) + jnp.sum(grad_low.astype(F32) * low.astype(F32), axis=1, keepdims=True)
            norm_grad = (dot_nt(grad_value, vw[...]) + dot_nt(grad_low, aw[...])) * gain[...]
            result = (
                dh[m].astype(F32)
                + scale * norm_grad
                - h[m].astype(F32) * (scale * scale * inner / hidden)
            ).astype(BF)

            @pl.when(m > 0)
            def _():
                wait_bytes(dh_out, send_sem.at[1])

            dh_out[...] = result
            remote(
                dh_out, dh.at[m], send_sem.at[1], dh_sem.at[m], {"section": s - 1}
            ).start()

        back.drain(m)

    @pl.when(s == 0)
    def _():
        for m in range(min(2, micros)):
            spread(tok, h, tok_sem, send_sem.at[2], m)

    part_rows = bpart.shape[0]
    up_place = pl.ds(pl.multiple_of(j * part_rows, part_rows), part_rows)

    def send_up(k, carry):
        remote(
            bpart, bw.at[up_place], send_sem.at[4], up_sem.at[0], {"dp": lax.rem(j + k, n)}
        ).start()
        return carry

    lax.fori_loop(1, n, send_up, 0)
    bw[up_place, :] = bpart[...]
    others = bw.at[pl.ds(0, (n - 1) * part_rows)]
    wait_bytes(others, up_sem.at[0])

    def step(t, carry):
        m_f = t - s
        m_b = t - (2 * sections - 1 - s)
        on_f = (m_f >= 0) & (m_f < micros)
        on_b = (m_b >= 0) & (m_b < micros)

        @pl.when((s == 0) & (t + 2 < micros))
        def _():
            spread(tok, h, tok_sem, send_sem.at[2], t + 2)

        @pl.when((s == last) & (t < micros))
        def _():
            spread(cot, dh, cot_sem, send_sem.at[3], t)

        pl.when(on_f)(lambda: ahead_start(m_f))
        pl.when(on_f)(lambda: ahead.scatter())
        pl.when(on_b)(lambda: back_start(m_b))
        pl.when(on_f)(lambda: ahead.gather(m_f))
        pl.when(on_b)(lambda: back.scatter())
        pl.when(on_f)(lambda: ahead.share(m_f))
        pl.when(on_b)(lambda: back.gather(m_b))
        pl.when(on_f)(lambda: ahead_end(m_f))
        pl.when(on_b)(lambda: back.share(m_b))
        pl.when(on_b)(lambda: back_end(m_b))
        return carry

    lax.fori_loop(0, micros + 2 * sections - 1, step, 0)

    wait_bytes(others, send_sem.at[4])

    @pl.when(s < last)
    def _():
        wait_bytes(h_out, send_sem.at[0])

    @pl.when(s > 0)
    def _():
        wait_bytes(dh_out, send_sem.at[1])

    @pl.when(s == 0)
    def _():
        wait_bytes(tok.at[:, pl.ds(0, (n - 1) * width)], send_sem.at[2])

    @pl.when(s == last)
    def _():
        wait_bytes(cot.at[:, pl.ds(0, (n - 1) * width)], send_sem.at[3])


def run_layers(tokens, cotangent, gain, vw, ow, aw, bw, mask, fold):
    sections, n = lax.axis_size("section"), lax.axis_size("dp")
    q = MROWS
    width, features = vw.shape
    ranks = aw.shape[1]
    micros = tokens.shape[0] // q
    rows = n * q
    wide = features + LANES
    vmem = pl.BlockSpec(memory_space=pltpu.VMEM)
    dma = pltpu.SemaphoreType.DMA
    dims = (sections, n, micros, q, features, width)
    return pl.pallas_call(
        functools.partial(layers_kernel, dims),
        out_shape=(
            jax.ShapeDtypeStruct((micros, rows, width), BF),
            jax.ShapeDtypeStruct((micros, rows, wide), BF),
            jax.ShapeDtypeStruct((micros, rows, features), BF),
            jax.ShapeDtypeStruct((micros, rows, ranks), BF),
        ),
        in_specs=[vmem] * 9,
        out_specs=(vmem,) * 4,
        scratch_shapes=[
            pltpu.VMEM((micros, rows, width), BF),
            pltpu.VMEM((ranks, features), BF),
            pltpu.VMEM((rows, wide), BF),
            pltpu.VMEM((rows // 2, wide), BF),
            pltpu.VMEM((rows // 2, wide), BF),
            pltpu.VMEM((n // 2, q, wide), BF),
            pltpu.VMEM((rows, features), BF),
            pltpu.VMEM((rows // 2, features), BF),
            pltpu.VMEM((rows // 2, features), BF),
            pltpu.VMEM((n // 2, q, features), BF),
            pltpu.VMEM((rows, width), BF),
            pltpu.VMEM((rows, width), BF),
            dma((8,)),
            dma((8,)),
            dma((micros,)),
            dma((micros,)),
            dma((micros,)),
            dma((micros,)),
            dma((1,)),
            dma((5,)),
        ],
        compiler_params=pltpu.CompilerParams(
            collective_id=0, has_side_effects=True, vmem_limit_bytes=58 * 1024 * 1024
        ),
    )(tokens, cotangent, gain, vw, ow, aw, bw, mask, fold)


def adam_update(params_old, first_old, second_old, slot_grad, live):
    first_step = BETA_FIRST * first_old + (1.0 - BETA_FIRST) * slot_grad
    second_step = BETA_SECOND * second_old + (1.0 - BETA_SECOND) * slot_grad * slot_grad
    step_size = first_step / FIRST_FIX / (jnp.sqrt(second_step / SECOND_FIX) + ADAM_EPS)
    params_step = (params_old.astype(jnp.float32) - LEARN_RATE * step_size).astype(jnp.bfloat16)
    return (
        jnp.where(live, params_step, params_old),
        jnp.where(live, first_step, first_old),
        jnp.where(live, second_step, second_old),
    )


def on_device(
    tokens,
    cotangent,
    gains,
    value_projection_weight,
    output_projection_weight,
    block_adapter_ids,
    job_adapter,
    job_slab,
    token_counts,
    slot_adapter_params,
    first_moment,
    second_moment,
):
    section_index = lax.axis_index("section")
    owner_index = lax.axis_index("dp")
    section_total = lax.axis_size("section")
    owner_total = lax.axis_size("dp")
    tok_dev, hidden_width = tokens.shape
    value_feature_width = value_projection_weight.shape[2]
    panel_width = slot_adapter_params.shape[2]
    slab_count = owner_total // 2
    block_total = block_adapter_ids.shape[0]
    local_blocks = block_total // owner_total
    block_rows = tok_dev // local_blocks
    adapter_total = token_counts.shape[0]
    divide_position = hidden_width * ADAPTER_RANK
    width = hidden_width // owner_total
    gain = lax.dynamic_slice_in_dim(gains, owner_index * width, width, axis=1)
    my_jobs = lax.dynamic_index_in_dim(job_adapter, owner_index, 0, keepdims=False)
    my_blocks = lax.dynamic_slice_in_dim(
        block_adapter_ids, owner_index * local_blocks, local_blocks
    )
    slab_ids = jnp.arange(slab_count, dtype=jnp.int32)
    matching = (job_adapter[None, None] == my_blocks[:, None, None, None]) & (
        job_slab[None, None] == slab_ids[None, :, None, None]
    )
    owner_ids = jnp.arange(owner_total, dtype=jnp.int32)
    source_owner = jnp.sum(jnp.where(matching, owner_ids[None, None, :, None], 0), axis=(2, 3))
    own_select = (block_adapter_ids[:, None] == my_jobs[None, :]) & (my_jobs[None, :] >= 0)
    slot_rows = jnp.arange(local_blocks, dtype=jnp.int32)[:, None]

    def hand_out(owned):
        picked = jnp.dot(own_select.astype(jnp.bfloat16), owned, preferred_element_type=jnp.float32)
        return picked.astype(jnp.bfloat16).reshape(owner_total, local_blocks, panel_width)

    def assemble(arrived):
        gathered_slabs = arrived[source_owner, slot_rows]
        return gathered_slabs.reshape(local_blocks, slab_count * panel_width)

    ranks = block_total * ADAPTER_RANK
    my_slabs = lax.dynamic_index_in_dim(job_slab, owner_index, 0, keepdims=False)
    held_slab = jnp.max(jnp.where(own_select, my_slabs[None, :], -1), axis=1)
    held = held_slab[:, None] == slab_ids[None, :]
    picked = hand_out(slot_adapter_params[0]).reshape(block_total, 1, panel_width)
    padded = jnp.where(held[:, :, None], picked, jnp.zeros((), BF)).reshape(
        block_total, slab_count * panel_width
    )
    down_part = jnp.transpose(
        padded[:, :divide_position].reshape(block_total, owner_total, width * ADAPTER_RANK),
        (1, 0, 2),
    )
    up_part = padded[:, divide_position:].reshape(owner_total, block_total, -1)
    owned_parts = lax.psum_scatter(
        jnp.concatenate([down_part, up_part], axis=2), "dp", scatter_dimension=0, tiled=False
    )
    adapter_up = owned_parts[:, width * ADAPTER_RANK :].reshape(-1, value_feature_width)
    adapter_down = jnp.transpose(
        owned_parts[:, : width * ADAPTER_RANK].reshape(block_total, width, ADAPTER_RANK),
        (1, 0, 2),
    ).reshape(width, ranks)
    rows = owner_total * MROWS
    mask = (
        jnp.arange(rows, dtype=jnp.int32)[:, None] // MROWS
        == jnp.arange(ranks, dtype=jnp.int32)[None, :] // ADAPTER_RANK
    )
    fold = (
        jnp.arange(ranks, dtype=jnp.int32)[:, None] % ADAPTER_RANK
        == jnp.arange(LANES, dtype=jnp.int32)[None, :]
    ).astype(BF)
    hidden, val, grad_value, grad_low = run_layers(
        tokens,
        cotangent,
        gain,
        value_projection_weight[0],
        output_projection_weight[0],
        adapter_down,
        adapter_up,
        mask.astype(F32),
        fold,
    )
    total_rows = hidden.shape[0] * rows
    tail = val[:, :, value_feature_width:]
    scale = tail[:, :, ADAPTER_RANK].astype(F32) + tail[:, :, ADAPTER_RANK + 1].astype(F32)
    normed = (hidden.astype(F32) * scale[:, :, None] * gain[0]).astype(BF)
    low = jnp.where(
        mask, jnp.tile(tail[:, :, :ADAPTER_RANK], (1, 1, block_total)), jnp.zeros((), BF)
    )
    down_grads = dot_tn(
        normed.reshape(total_rows, width), grad_low.reshape(total_rows, ranks)
    ).astype(BF)
    up_grads = (
        ADAPTER_SCALE
        * dot_tn(
            low.reshape(total_rows, ranks), grad_value.reshape(total_rows, value_feature_width)
        )
    ).astype(BF)
    down_grads = jnp.transpose(
        down_grads.reshape(width, block_total, ADAPTER_RANK), (1, 0, 2)
    ).reshape(block_total, width * ADAPTER_RANK)
    down_grads = lax.all_gather(down_grads, "dp", axis=1, tiled=True)
    block_grads = jnp.concatenate(
        [down_grads, up_grads.reshape(block_total, ADAPTER_RANK * value_feature_width)], axis=1
    ).reshape(block_total, slab_count, panel_width)
    arrived = jnp.sum(
        jnp.where(held[:, :, None], block_grads.astype(F32), 0.0), axis=1
    ).astype(BF)
    summed = dot_tn(own_select.astype(BF), arrived)
    live = my_jobs >= 0
    adapter_ids = jnp.arange(adapter_total, dtype=jnp.int32)
    slot_counts = jnp.sum(
        jnp.where(adapter_ids[None, :] == my_jobs[:, None], token_counts[None, :], 0), axis=1
    )
    slot_counts = jnp.where(live, slot_counts, 1)
    slot_grad = summed / slot_counts.astype(jnp.float32)[:, None]
    slot_of_block = jnp.argmax(own_select, axis=1)
    block_params, _, _ = adam_update(
        slot_adapter_params[0][slot_of_block],
        first_moment[0][slot_of_block],
        second_moment[0][slot_of_block],
        slot_grad[slot_of_block],
        jnp.any(own_select, axis=1)[:, None],
    )
    returned = assemble(
        lax.all_to_all(
            block_params.reshape(owner_total, local_blocks, panel_width),
            "dp",
            split_axis=0,
            concat_axis=0,
            tiled=True,
        )
    )
    params_new, first_new, second_new = adam_update(
        slot_adapter_params[0], first_moment[0], second_moment[0], slot_grad, live[:, None]
    )
    return (params_new[None], first_new[None], second_new[None], returned[None])


def solution(mesh):
    return jax.shard_map(
        on_device,
        mesh=mesh,
        in_specs=(
            P("dp", None),
            P("dp", None),
            P("section", None),
            P("section", "dp", None),
            P("section", "dp", None),
            P(),
            P(),
            P(),
            P(),
            P("section", "dp", None),
            P("section", "dp", None),
            P("section", "dp", None),
        ),
        out_specs=(
            P("section", "dp", None),
            P("section", "dp", None),
            P("section", "dp", None),
            P("section", "dp", None),
        ),
        check_vma=False,
    )
```

```python
import functools

import jax
import jax.numpy as jnp
from jax import lax
from jax.experimental import pallas as pl
from jax.experimental.pallas import tpu as pltpu
from jax.sharding import PartitionSpec as P

ADAPTER_RANK = 16
MROWS = 16
LANES = 128


ADAPTER_SCALE = 2.0
LEARN_RATE = 0.001
BETA_FIRST = 0.9
BETA_SECOND = 0.999
ADAM_EPS = 1e-08
FIRST_FIX = 1.0 - 0.9**50 * 0.9**50
SECOND_FIX = 1.0 - 0.999**50 * 0.999**50
NORM_EPS = 1e-05
MESH = pl.DeviceIdType.MESH
BF = jnp.bfloat16
F32 = jnp.float32


def dot_nt(left, right):
    return lax.dot_general(left, right, (((1,), (1,)), ((), ())), preferred_element_type=F32)


def dot_tn(left, right):
    return lax.dot_general(left, right, (((0,), (0,)), ((), ())), preferred_element_type=F32)


def dot_nn(left, right):
    return jnp.dot(left, right, preferred_element_type=F32)


def layers_kernel(
    dims,
    tok,
    cot,
    gain,
    vw,
    ow,
    aw,
    bpart,
    mask,
    fold,
    vt,
    ot,
    at,
    unfold,
    h,
    val,
    gv,
    gl,
    dh,
    bw,
    bt,
    snd_f,
    pr_f,
    mid_f,
    rs_f,
    snd_b,
    pr_b,
    mid_b,
    rs_b,
    h_out,
    dh_out,
    sem_f,
    sem_b,
    h_sem,
    dh_sem,
    tok_sem,
    cot_sem,
    up_sem,
    send_sem,
):
    sections, n, micros, q, features, width = dims
    hz = n // 2
    rows = n * q
    half = rows // 2
    hidden = n * width
    s = lax.axis_index("section")
    j = lax.axis_index("dp")
    z = j // 2
    c = lax.rem(j, 2)
    peer = j + 1 - 2 * c
    last = sections - 1

    barrier = pltpu.get_barrier_semaphore()

    def greet(k, carry):
        pl.semaphore_signal(
            barrier, inc=1, device_id={"dp": lax.rem(j + k, n)}, device_id_type=MESH
        )
        return carry

    lax.fori_loop(1, n, greet, 0)

    @pl.when(s > 0)
    def _():
        pl.semaphore_signal(barrier, inc=1, device_id={"section": s - 1}, device_id_type=MESH)

    @pl.when(s < last)
    def _():
        pl.semaphore_signal(barrier, inc=1, device_id={"section": s + 1}, device_id_type=MESH)

    beside = jnp.where(s > 0, 1, 0) + jnp.where(s < last, 1, 0)
    pl.semaphore_wait(barrier, n - 1 + beside)

    def remote(source, target, send, recv, device):
        return pltpu.make_async_remote_copy(
            src_ref=source,
            dst_ref=target,
            send_sem=send,
            recv_sem=recv,
            device_id=device,
            device_id_type=MESH,
        )

    def wait_bytes(ref, sem):
        pltpu.make_async_copy(ref, ref, sem).wait()

    def spread(source, target, sem, sent, m):
        mine = pl.ds(pl.multiple_of(m * q, q), q)
        place = pl.ds(pl.multiple_of(j * q, q), q)

        def one(k, carry):
            to = lax.rem(j + k, n)
            columns = pl.ds(pl.multiple_of(to * width, width), width)
            remote(
                source.at[mine, columns], target.at[m, place], sent, sem.at[m], {"dp": to}
            ).start()
            return carry

        lax.fori_loop(1, n, one, 0)
        target[m, place, :] = source[mine, pl.ds(pl.multiple_of(j * width, width), width)]

    def spread_wait(target, sem, m):
        wait_bytes(target.at[m, pl.ds(0, (n - 1) * q)], sem.at[m])

    class Reduce:
        def __init__(self, snd, pr, mid, rs, out, sem, middle, finish):
            self.snd, self.pr, self.mid, self.rs = snd, pr, mid, rs
            self.out, self.sem, self.middle, self.finish = out, sem, middle, finish
            self.own = pl.ds(pl.multiple_of(c * half, half), half)
            self.other = pl.ds(pl.multiple_of((1 - c) * half, half), half)
            self.chunk = pl.ds(pl.multiple_of(c * half + z * q, q), q)

        def pair(self):
            return remote(
                self.snd.at[self.other], self.pr, self.sem.at[0], self.sem.at[1], {"dp": peer}
            )

        def scatter(self):
            self.pair().wait_recv()
            total = self.snd[self.own, :].astype(F32) + self.pr[...].astype(F32)
            self.mid[...] = self.middle(total)
            for k in range(1, hz):
                to = lax.rem(z + k, hz)
                remote(
                    self.mid.at[pl.ds(pl.multiple_of(to * q, q), q)],
                    self.rs.at[z],
                    self.sem.at[2],
                    self.sem.at[3],
                    {"dp": 2 * to + c},
                ).start()
            self.rs[z] = self.mid[pl.ds(pl.multiple_of(z * q, q), q), :]

        def gather(self, m):
            if hz > 1:
                wait_bytes(self.rs.at[pl.ds(0, hz - 1)], self.sem.at[3])
            total = self.rs[0].astype(F32)
            for k in range(1, hz):
                total = total + self.rs[k].astype(F32)
            self.out[m, self.chunk, :] = self.finish(total)
            for k in range(1, hz):
                to = lax.rem(z + k, hz)
                remote(
                    self.out.at[m, self.chunk],
                    self.out.at[m, self.chunk],
                    self.sem.at[4],
                    self.sem.at[5],
                    {"dp": 2 * to + c},
                ).start()

        def share(self, m):
            if hz > 1:
                wait_bytes(self.out.at[m, pl.ds(0, (hz - 1) * q)], self.sem.at[5])
            remote(
                self.out.at[m, self.own],
                self.out.at[m, self.own],
                self.sem.at[6],
                self.sem.at[7],
                {"dp": peer},
            ).start()

        def arrive(self, m):
            wait_bytes(self.out.at[m, pl.ds(0, half)], self.sem.at[7])

        def drain(self, m):
            self.pair().wait_send()
            if hz > 1:
                wait_bytes(self.mid.at[pl.ds(0, (hz - 1) * q)], self.sem.at[2])
                wait_bytes(self.out.at[m, pl.ds(0, (hz - 1) * q)], self.sem.at[4])
            wait_bytes(self.out.at[m, pl.ds(0, half)], self.sem.at[6])

    def with_stat(tail, stat):
        spot = lax.broadcasted_iota(jnp.int32, tail.shape, 1)
        high = stat.astype(BF).astype(F32)
        rest = stat - high
        return jnp.where(
            spot < ADAPTER_RANK,
            tail,
            jnp.where(
                spot == ADAPTER_RANK, high, jnp.where(spot == ADAPTER_RANK + 1, rest, 0.0)
            ),
        ).astype(BF)

    def stat_of(tail):
        spot = lax.broadcasted_iota(jnp.int32, tail.shape, 1)
        inside = (spot == ADAPTER_RANK) | (spot == ADAPTER_RANK + 1)
        return jnp.sum(jnp.where(inside, tail, 0.0), axis=1, keepdims=True)

    def middle_f(total):
        tail = total[:, features:]
        return jnp.concatenate(
            [total[:, :features].astype(BF), with_stat(tail, stat_of(tail))], axis=1
        )

    def finish_f(total):
        tail = total[:, features:]
        scale = lax.rsqrt(stat_of(tail) / hidden + NORM_EPS)
        return jnp.concatenate(
            [(total[:, :features] * scale).astype(BF), with_stat(tail * scale, scale)], axis=1
        )

    def plain(total):
        return total.astype(BF)

    ahead = Reduce(snd_f, pr_f, mid_f, rs_f, val, sem_f, middle_f, finish_f)
    back = Reduce(snd_b, pr_b, mid_b, rs_b, gv, sem_b, plain, plain)

    def wide_low(tail):
        spread_low = dot_nn(tail, unfold[...])
        return jnp.where(mask[...] > 0, spread_low, 0.0).astype(BF)

    def ahead_start(m):
        @pl.when(s == 0)
        def _():
            spread_wait(h, tok_sem, m)

        @pl.when(s > 0)
        def _():
            wait_bytes(h.at[m], h_sem.at[m])

        wide = h[m].astype(F32)
        scaled = (wide * gain[...]).astype(BF)
        snd_f[:, :features] = dot_nn(scaled, vw[...]).astype(BF)
        low = jnp.where(mask[...] > 0, dot_nn(scaled, aw[...]), 0.0).astype(BF)
        squares = jnp.sum(wide * wide, axis=1, keepdims=True)
        snd_f[:, features:] = with_stat(dot_nn(low, fold[...]), squares)
        ahead.pair().start()

    def ahead_end(m):
        ahead.arrive(m)

        @pl.when(s < last)
        def _():
            low = wide_low(val[m, :, features:])
            value = (
                val[m, :, :features].astype(F32) + ADAPTER_SCALE * dot_nn(low, bw[...])
            ).astype(BF)
            result = (h[m].astype(F32) + dot_nn(value, ot[...])).astype(BF)

            @pl.when(m > 0)
            def _():
                wait_bytes(h_out, send_sem.at[0])

            h_out[...] = result
            remote(
                h_out, h.at[m], send_sem.at[0], h_sem.at[m], {"section": s + 1}
            ).start()

        ahead.drain(m)

    def back_start(m):
        @pl.when(s == last)
        def _():
            spread_wait(dh, cot_sem, m)

        @pl.when(s < last)
        def _():
            wait_bytes(dh.at[m], dh_sem.at[m])

        snd_b[...] = dot_nn(dh[m], ow[...]).astype(BF)
        back.pair().start()

    def back_end(m):
        back.arrive(m)
        grad_value = gv[m]
        grad_low = jnp.where(
            mask[...] > 0, ADAPTER_SCALE * dot_nn(grad_value, bt[...]), 0.0
        ).astype(BF)
        gl[m] = grad_low

        @pl.when(s > 0)
        def _():
            tail = val[m, :, features:]
            scale = stat_of(tail.astype(F32))
            low = wide_low(tail)
            inner = jnp.sum(
                grad_value.astype(F32) * val[m, :, :features].astype(F32), axis=1, keepdims=True
            ) + jnp.sum(grad_low.astype(F32) * low.astype(F32), axis=1, keepdims=True)
            norm_grad = (dot_nn(grad_value, vt[...]) + dot_nn(grad_low, at[...])) * gain[...]
            result = (
                dh[m].astype(F32)
                + scale * norm_grad
                - h[m].astype(F32) * (scale * scale * inner / hidden)
            ).astype(BF)

            @pl.when(m > 0)
            def _():
                wait_bytes(dh_out, send_sem.at[1])

            dh_out[...] = result
            remote(
                dh_out, dh.at[m], send_sem.at[1], dh_sem.at[m], {"section": s - 1}
            ).start()

        back.drain(m)

    @pl.when(s == 0)
    def _():
        for m in range(min(2, micros)):
            spread(tok, h, tok_sem, send_sem.at[2], m)

    part_rows = bpart.shape[0]
    up_place = pl.ds(pl.multiple_of(j * part_rows, part_rows), part_rows)

    def send_up(k, carry):
        remote(
            bpart, bw.at[up_place], send_sem.at[4], up_sem.at[0], {"dp": lax.rem(j + k, n)}
        ).start()
        return carry

    lax.fori_loop(1, n, send_up, 0)
    bw[up_place, :] = bpart[...]
    others = bw.at[pl.ds(0, (n - 1) * part_rows)]
    wait_bytes(others, up_sem.at[0])
    bt[...] = bw[...].astype(F32).T.astype(BF)

    def step(t, carry):
        m_f = t - s
        m_b = t - (2 * sections - 1 - s)
        on_f = (m_f >= 0) & (m_f < micros)
        on_b = (m_b >= 0) & (m_b < micros)

        @pl.when((s == 0) & (t + 2 < micros))
        def _():
            spread(tok, h, tok_sem, send_sem.at[2], t + 2)

        @pl.when((s == last) & (t < micros))
        def _():
            spread(cot, dh, cot_sem, send_sem.at[3], t)

        pl.when(on_f)(lambda: ahead_start(m_f))
        pl.when(on_f)(lambda: ahead.scatter())
        pl.when(on_b)(lambda: back_start(m_b))
        pl.when(on_f)(lambda: ahead.gather(m_f))
        pl.when(on_b)(lambda: back.scatter())
        pl.when(on_f)(lambda: ahead.share(m_f))
        pl.when(on_b)(lambda: back.gather(m_b))
        pl.when(on_f)(lambda: ahead_end(m_f))
        pl.when(on_b)(lambda: back.share(m_b))
        pl.when(on_b)(lambda: back_end(m_b))
        return carry

    lax.fori_loop(0, micros + 2 * sections - 1, step, 0)

    wait_bytes(others, send_sem.at[4])

    @pl.when(s < last)
    def _():
        wait_bytes(h_out, send_sem.at[0])

    @pl.when(s > 0)
    def _():
        wait_bytes(dh_out, send_sem.at[1])

    @pl.when(s == 0)
    def _():
        wait_bytes(tok.at[:, pl.ds(0, (n - 1) * width)], send_sem.at[2])

    @pl.when(s == last)
    def _():
        wait_bytes(cot.at[:, pl.ds(0, (n - 1) * width)], send_sem.at[3])


def run_layers(tokens, cotangent, gain, vw, ow, aw, bw, mask, fold, at):
    sections, n = lax.axis_size("section"), lax.axis_size("dp")
    q = MROWS
    width, features = vw.shape
    ranks = aw.shape[1]
    micros = tokens.shape[0] // q
    rows = n * q
    wide = features + LANES
    vmem = pl.BlockSpec(memory_space=pltpu.VMEM)
    dma = pltpu.SemaphoreType.DMA
    dims = (sections, n, micros, q, features, width)
    return pl.pallas_call(
        functools.partial(layers_kernel, dims),
        out_shape=(
            jax.ShapeDtypeStruct((micros, rows, width), BF),
            jax.ShapeDtypeStruct((micros, rows, wide), BF),
            jax.ShapeDtypeStruct((micros, rows, features), BF),
            jax.ShapeDtypeStruct((micros, rows, ranks), BF),
        ),
        in_specs=[vmem] * 13,
        out_specs=(vmem,) * 4,
        scratch_shapes=[
            pltpu.VMEM((micros, rows, width), BF),
            pltpu.VMEM((ranks, features), BF),
            pltpu.VMEM((features, ranks), BF),
            pltpu.VMEM((rows, wide), BF),
            pltpu.VMEM((rows // 2, wide), BF),
            pltpu.VMEM((rows // 2, wide), BF),
            pltpu.VMEM((n // 2, q, wide), BF),
            pltpu.VMEM((rows, features), BF),
            pltpu.VMEM((rows // 2, features), BF),
            pltpu.VMEM((rows // 2, features), BF),
            pltpu.VMEM((n // 2, q, features), BF),
            pltpu.VMEM((rows, width), BF),
            pltpu.VMEM((rows, width), BF),
            dma((8,)),
            dma((8,)),
            dma((micros,)),
            dma((micros,)),
            dma((micros,)),
            dma((micros,)),
            dma((1,)),
            dma((5,)),
        ],
        compiler_params=pltpu.CompilerParams(
            collective_id=0, has_side_effects=True, vmem_limit_bytes=58 * 1024 * 1024
        ),
    )(tokens, cotangent, gain, vw, ow, aw, bw, mask, fold, vw.T, ow.T, at, fold.T)


def adam_kernel(own, counts, live, arrived, params, first, second, params_out, first_out, second_out):
    slot_grad = dot_nn(own[...], arrived[...]) / counts[...]
    on = live[...] > 0
    first_old, second_old = first[...], second[...]
    params_old = params[...].astype(F32)
    first_step = BETA_FIRST * first_old + (1.0 - BETA_FIRST) * slot_grad
    second_step = BETA_SECOND * second_old + (1.0 - BETA_SECOND) * slot_grad * slot_grad
    step_size = first_step / FIRST_FIX / (jnp.sqrt(second_step / SECOND_FIX) + ADAM_EPS)
    params_out[...] = jnp.where(on, params_old - LEARN_RATE * step_size, params_old).astype(BF)
    first_out[...] = jnp.where(on, first_step, first_old)
    second_out[...] = jnp.where(on, second_step, second_old)


def run_adam(own, counts, live, arrived, params, first, second):
    slots, panel = params.shape
    blocks = arrived.shape[0]
    tile = max(k for k in range(128, 4609, 128) if panel % k == 0)

    def whole(*shape):
        return pl.BlockSpec(shape, lambda i: (0, 0))

    def cut(count):
        return pl.BlockSpec((count, tile), lambda i: (0, i))

    return pl.pallas_call(
        adam_kernel,
        grid=(panel // tile,),
        out_shape=(
            jax.ShapeDtypeStruct((slots, panel), BF),
            jax.ShapeDtypeStruct((slots, panel), F32),
            jax.ShapeDtypeStruct((slots, panel), F32),
        ),
        in_specs=[
            whole(slots, blocks),
            whole(slots, 1),
            whole(slots, 1),
            cut(blocks),
            cut(slots),
            cut(slots),
            cut(slots),
        ],
        out_specs=(cut(slots),) * 3,
        compiler_params=pltpu.CompilerParams(vmem_limit_bytes=48 * 1024 * 1024),
        cost_estimate=pl.CostEstimate(
            flops=20 * slots * panel, bytes_accessed=20 * slots * panel, transcendentals=0
        ),
    )(own, counts, live, arrived, params, first, second)


def adam_update(params_old, first_old, second_old, slot_grad, live):
    first_step = BETA_FIRST * first_old + (1.0 - BETA_FIRST) * slot_grad
    second_step = BETA_SECOND * second_old + (1.0 - BETA_SECOND) * slot_grad * slot_grad
    step_size = first_step / FIRST_FIX / (jnp.sqrt(second_step / SECOND_FIX) + ADAM_EPS)
    params_step = (params_old.astype(jnp.float32) - LEARN_RATE * step_size).astype(jnp.bfloat16)
    return (
        jnp.where(live, params_step, params_old),
        jnp.where(live, first_step, first_old),
        jnp.where(live, second_step, second_old),
    )


def on_device(
    tokens,
    cotangent,
    gains,
    value_projection_weight,
    output_projection_weight,
    block_adapter_ids,
    job_adapter,
    job_slab,
    token_counts,
    slot_adapter_params,
    first_moment,
    second_moment,
):
    section_index = lax.axis_index("section")
    owner_index = lax.axis_index("dp")
    section_total = lax.axis_size("section")
    owner_total = lax.axis_size("dp")
    tok_dev, hidden_width = tokens.shape
    value_feature_width = value_projection_weight.shape[2]
    panel_width = slot_adapter_params.shape[2]
    slab_count = owner_total // 2
    block_total = block_adapter_ids.shape[0]
    local_blocks = block_total // owner_total
    block_rows = tok_dev // local_blocks
    adapter_total = token_counts.shape[0]
    divide_position = hidden_width * ADAPTER_RANK
    width = hidden_width // owner_total
    gain = lax.dynamic_slice_in_dim(gains, owner_index * width, width, axis=1)
    my_jobs = lax.dynamic_index_in_dim(job_adapter, owner_index, 0, keepdims=False)
    my_blocks = lax.dynamic_slice_in_dim(
        block_adapter_ids, owner_index * local_blocks, local_blocks
    )
    slab_ids = jnp.arange(slab_count, dtype=jnp.int32)
    matching = (job_adapter[None, None] == my_blocks[:, None, None, None]) & (
        job_slab[None, None] == slab_ids[None, :, None, None]
    )
    owner_ids = jnp.arange(owner_total, dtype=jnp.int32)
    source_owner = jnp.sum(jnp.where(matching, owner_ids[None, None, :, None], 0), axis=(2, 3))
    own_select = (block_adapter_ids[:, None] == my_jobs[None, :]) & (my_jobs[None, :] >= 0)
    slot_rows = jnp.arange(local_blocks, dtype=jnp.int32)[:, None]

    def hand_out(owned):
        picked = jnp.dot(own_select.astype(jnp.bfloat16), owned, preferred_element_type=jnp.float32)
        return picked.astype(jnp.bfloat16).reshape(owner_total, local_blocks, panel_width)

    def assemble(arrived):
        gathered_slabs = arrived[source_owner, slot_rows]
        return gathered_slabs.reshape(local_blocks, slab_count * panel_width)

    ranks = block_total * ADAPTER_RANK
    my_slabs = lax.dynamic_index_in_dim(job_slab, owner_index, 0, keepdims=False)
    held_slab = jnp.max(jnp.where(own_select, my_slabs[None, :], -1), axis=1)
    held = held_slab[:, None] == slab_ids[None, :]
    picked = hand_out(slot_adapter_params[0]).reshape(block_total, 1, panel_width)
    padded = jnp.where(held[:, :, None], picked, jnp.zeros((), BF)).reshape(
        block_total, slab_count * panel_width
    )
    down_part = jnp.transpose(
        padded[:, :divide_position].reshape(block_total, owner_total, width * ADAPTER_RANK),
        (1, 0, 2),
    )
    up_part = padded[:, divide_position:].reshape(owner_total, block_total, -1)
    owned_parts = lax.psum_scatter(
        jnp.concatenate([down_part, up_part], axis=2), "dp", scatter_dimension=0, tiled=False
    )
    adapter_up = owned_parts[:, width * ADAPTER_RANK :].reshape(-1, value_feature_width)
    down_turned = jnp.transpose(
        owned_parts[:, : width * ADAPTER_RANK].reshape(block_total, width, ADAPTER_RANK),
        (0, 2, 1),
    ).reshape(ranks, width)
    adapter_down = down_turned.T
    rows = owner_total * MROWS
    mask = (
        jnp.arange(rows, dtype=jnp.int32)[:, None] // MROWS
        == jnp.arange(ranks, dtype=jnp.int32)[None, :] // ADAPTER_RANK
    )
    fold = (
        jnp.arange(ranks, dtype=jnp.int32)[:, None] % ADAPTER_RANK
        == jnp.arange(LANES, dtype=jnp.int32)[None, :]
    ).astype(BF)
    hidden, val, grad_value, grad_low = run_layers(
        tokens,
        cotangent,
        gain,
        value_projection_weight[0],
        output_projection_weight[0],
        adapter_down,
        adapter_up,
        mask.astype(F32),
        fold,
        down_turned,
    )
    total_rows = hidden.shape[0] * rows
    tail = val[:, :, value_feature_width:]
    scale = tail[:, :, ADAPTER_RANK].astype(F32) + tail[:, :, ADAPTER_RANK + 1].astype(F32)
    normed = (hidden.astype(F32) * scale[:, :, None] * gain[0]).astype(BF)
    low = jnp.where(
        mask, jnp.tile(tail[:, :, :ADAPTER_RANK], (1, 1, block_total)), jnp.zeros((), BF)
    )
    down_grads = dot_tn(
        normed.reshape(total_rows, width), grad_low.reshape(total_rows, ranks)
    ).astype(BF)
    up_grads = (
        ADAPTER_SCALE
        * dot_tn(
            low.reshape(total_rows, ranks), grad_value.reshape(total_rows, value_feature_width)
        )
    ).astype(BF)
    down_grads = jnp.transpose(
        down_grads.reshape(width, block_total, ADAPTER_RANK), (1, 0, 2)
    ).reshape(block_total, width * ADAPTER_RANK)
    down_grads = lax.all_gather(down_grads, "dp", axis=1, tiled=True)
    block_grads = jnp.concatenate(
        [down_grads, up_grads.reshape(block_total, ADAPTER_RANK * value_feature_width)], axis=1
    ).reshape(block_total, slab_count, panel_width)
    arrived = jnp.sum(jnp.where(held[:, :, None], block_grads.astype(F32), 0.0), axis=1)
    same = (block_adapter_ids[:, None] == block_adapter_ids[None, :]).astype(F32)
    block_grad = dot_nn(same, arrived) / token_counts[block_adapter_ids].astype(F32)[:, None]
    live = my_jobs >= 0
    adapter_ids = jnp.arange(adapter_total, dtype=jnp.int32)
    slot_counts = jnp.sum(
        jnp.where(adapter_ids[None, :] == my_jobs[:, None], token_counts[None, :], 0), axis=1
    )
    slot_counts = jnp.where(live, slot_counts, 1)
    slot_of_block = jnp.argmax(own_select, axis=1)
    block_params, _, _ = adam_update(
        slot_adapter_params[0][slot_of_block],
        first_moment[0][slot_of_block],
        second_moment[0][slot_of_block],
        block_grad,
        jnp.any(own_select, axis=1)[:, None],
    )
    returned = assemble(
        lax.all_to_all(
            block_params.reshape(owner_total, local_blocks, panel_width),
            "dp",
            split_axis=0,
            concat_axis=0,
            tiled=True,
        )
    )
    params_new, first_new, second_new = run_adam(
        own_select.astype(F32).T,
        slot_counts.astype(F32)[:, None],
        live.astype(F32)[:, None],
        arrived,
        slot_adapter_params[0],
        first_moment[0],
        second_moment[0],
    )
    return (params_new[None], first_new[None], second_new[None], returned[None])


def solution(mesh):
    return jax.shard_map(
        on_device,
        mesh=mesh,
        in_specs=(
            P("dp", None),
            P("dp", None),
            P("section", None),
            P("section", "dp", None),
            P("section", "dp", None),
            P(),
            P(),
            P(),
            P(),
            P("section", "dp", None),
            P("section", "dp", None),
            P("section", "dp", None),
        ),
        out_specs=(
            P("section", "dp", None),
            P("section", "dp", None),
            P("section", "dp", None),
            P("section", "dp", None),
        ),
        check_vma=False,
    )
```
